32 devices in a mesh: groups: 2 (over y), heads: 4 (over z), rows: 4 (over x, core).
Axes of the slice: x: 2, y: 2, z: 4, core: 2. Of those that a mesh axis runs over, the one named last changes fastest.
Arguments:
- queries: bfloat16 [512, 8192], P(('groups', 'heads')), parts along dimension 0, may hold values from -7 to 7
- kv_cache: bfloat16 [2, 4, 16384, 128], P(None, 'groups', ('heads', 'rows')), parts along dimension 1, may hold values from -7 to 7
- start_positions: int32 [4], P('groups'), parts along dimension 0, may hold values from 1024 to 1920, as said below
- residual: bfloat16 [512, 8192], P(('groups', 'heads'), 'rows'), parts along dimension 0, may hold values from -3 to 3
- out_weight: bfloat16 [8192, 8192], P('heads', 'rows'), may hold values from -2 to 2
- norm_gain: float32 [8192], P('rows'), may hold values from 0.1 to 1.9
- gate_weight: bfloat16 [8192, 14336], P('rows', 'heads'), may hold values from -0.0625 to 0.0625
- up_weight: bfloat16 [8192, 14336], P('rows', 'heads'), may hold values from -0.0625 to 0.0625
- down_weight: bfloat16 [14336, 8192], P('heads', 'rows'), may hold values from -0.046875 to 0.046875
Outputs:
- layer_out: bfloat16 [512, 8192], P(('groups', 'heads'), 'rows'), parts along dimension 0
The draws below stay inside these ranges and needn't reach their ends.
There are 2 independent parts, one for each index of `groups`. The reference program is written for one: setup_inputs(seed, part) draws one part's arguments, and reference() takes and returns one part's arrays. A program takes and returns all parts, laid end to end along the dimension named above; an argument that names none is the same for every part. Nothing has to cross between parts.
Inputs may be any that keep to these rules, and one draw needn't show every extreme that they name: Row s * 128 + t of queries is the token at position start_positions[s] + t of sequence s, and the keys and values of the new tokens already stand at those positions of kv_cache; some sequence starts at exactly 1920.
All inputs are finite; a program needn't handle non-finite values.
Results may differ from the reference program's by a relative error of at most 0.017.
Values may be sent and summed in bfloat16 or wider, within the bound.
A program may use at most 128 MiB of HBM per device.

```python
import math
import jax
import jax.numpy as jnp
from jax import lax

D = 8192
QH = 64
KVH = 8
HD = 128
FF = 14336
SEQS = 2
NEW = 128
ROWS = 256
CACHE = 2048


def shared_parts(key):
    base_key = jax.random.fold_in(key, 9001)
    start_key, pick_key, common_key, sign_key = jax.random.split(base_key, 4)
    lowest = jax.random.randint(start_key, (SEQS,), CACHE // 2, CACHE - NEW + 1)
    fullest = jax.random.randint(pick_key, (), 0, SEQS)
    starts = jnp.where(jnp.arange(SEQS) == fullest, CACHE - NEW, lowest).astype(jnp.int32)
    common = jnp.clip(jax.random.normal(common_key, (SEQS * NEW, KVH, HD), jnp.float32), -3.0, 3.0)
    sign_table = (2 * jax.random.randint(sign_key, (KVH, HD), 0, 2) - 1).astype(jnp.float32)
    return (starts, common, sign_table)


def draw_start_positions(key, part):
    return shared_parts(key)[0]


def draw_queries(key, part):
    common, sign_table = shared_parts(key)[1:]
    own_key = jax.random.fold_in(key, 1)
    group_size = QH // KVH
    own_part = jnp.clip(jax.random.normal(own_key, (SEQS * NEW, QH, HD), jnp.float32), -3.0, 3.0)
    mixed = 1.5 * (0.75 * own_part + 0.66 * jnp.repeat(common, group_size, axis=1))
    return mixed.reshape(SEQS * NEW, QH * HD).astype(jnp.bfloat16)


def draw_kv_cache(key, part):
    starts, common, sign_table = shared_parts(key)
    noise_key = jax.random.fold_in(key, 2)
    full_shape = (2, SEQS, KVH, CACHE, HD)
    noise = jnp.clip(jax.random.normal(noise_key, full_shape, jnp.float32), -3.0, 3.0)
    positions = jnp.arange(CACHE)
    offset = positions[None, :] - starts[:, None]
    inside = (offset >= 0) & (offset < NEW)
    source = jnp.clip(offset, 0, NEW - 1) + (jnp.arange(SEQS) * NEW)[:, None]
    own_part = jnp.transpose(common[source], (0, 2, 1, 3))
    key_rows = jnp.where(inside[:, None, :, None], 0.75 * noise[0] + 0.66 * own_part, noise[0])
    stacked = jnp.stack([1.5 * key_rows, noise[1]])
    return stacked.reshape(2, SEQS, KVH * CACHE, HD).astype(jnp.bfloat16)


def draw_residual(key, part):
    noise_key, row_key, col_key = jax.random.split(jax.random.fold_in(key, 4), 3)
    column = jnp.arange(D, dtype=jnp.float32) / D
    noise = jnp.clip(jax.random.normal(noise_key, (ROWS, D), jnp.float32), -3.0, 3.0)
    rising = 3.0 ** (column - 1.0)
    row_scale = jnp.exp(jax.random.uniform(row_key, (ROWS, 1), jnp.float32, math.log(0.1), 0.0))
    col_scale = rising * jnp.exp(jax.random.uniform(col_key, (D,), jnp.float32, math.log(0.3), 0.0))
    return (noise * row_scale * col_scale[None, :]).astype(jnp.bfloat16)


def draw_out_weight(key, part):
    noise_key = jax.random.fold_in(key, 5)
    column = jnp.arange(D, dtype=jnp.float32) / D
    noise = jnp.clip(jax.random.normal(noise_key, (QH * HD, D), jnp.float32), -4.0, 4.0)
    rising = 3.0 ** (column - 0.5)
    return (noise * rising[None, :] * math.sqrt(64.0 / (QH * HD))).astype(jnp.bfloat16)


def block_levels(rng, shape, cuts, smallest, largest):
    level = 1.0
    for axis_at, shards_of in cuts:
        draws = jax.random.uniform(jax.random.fold_in(jax.random.fold_in(rng, 6), axis_at), (shards_of,), jnp.float32, smallest / len(cuts), largest / len(cuts))
        level = level * jnp.repeat(jnp.exp(draws), shape[axis_at] // shards_of).reshape((-1,) + (1,) * (len(shape) - 1 - axis_at))
    return level


def normal_values(key, extent, scale, reach, cuts=(), kind=jnp.bfloat16):
    array = jax.random.normal(key, extent, jnp.float32) * scale
    if len(cuts) > 0:
        array = block_levels(key, extent, cuts, -0.22, 0.18) * array
    return jnp.clip(array, min=-reach, max=reach).astype(kind)


def setup_inputs(seed: int = 0, part: int = 0) -> dict:
    keys = jax.random.split(jax.random.key(seed), 10)
    part_splits = jax.random.split(jax.random.fold_in(keys[9], part), 10)
    queries = draw_queries(jax.random.fold_in(jax.random.fold_in(keys[9], part), 71), part)
    kv_cache = draw_kv_cache(jax.random.fold_in(jax.random.fold_in(keys[9], part), 71), part)
    start_positions = draw_start_positions(jax.random.fold_in(jax.random.fold_in(keys[9], part), 71), part)
    residual = draw_residual(jax.random.fold_in(jax.random.fold_in(keys[9], part), 71), part)
    out_weight = draw_out_weight(jax.random.fold_in(keys[9], 71), part)
    norm_gain = jnp.clip(1.0 + 0.18 * jax.random.normal(keys[5], (D,), jnp.float32), 0.1, 1.9)
    gate_weight = normal_values(keys[6], (D, FF), D ** -0.5, 0.0625, ((0, 4), (1, 4)))
    up_weight = normal_values(keys[7], (D, FF), D ** -0.5, 0.0625, ((0, 4), (1, 4)))
    down_weight = normal_values(keys[8], (FF, D), FF ** -0.5, 0.046875, ((0, 4), (1, 4)))
    return dict(queries=queries, kv_cache=kv_cache, start_positions=start_positions, residual=residual, out_weight=out_weight, norm_gain=norm_gain, gate_weight=gate_weight, up_weight=up_weight, down_weight=down_weight)


def attend_sequence(query_rows, cache_keys, cache_values, last_valid):
    group_size = QH // KVH
    score_scale = 1.0 / math.sqrt(HD)
    positions = jnp.arange(CACHE, dtype=jnp.int32)
    allowed = positions[None, :] <= last_valid[:, None]
    grouped = jnp.transpose(query_rows.reshape(NEW, KVH, group_size, HD), (1, 0, 2, 3))

    def one_group(operands):
        query_group, key_group, value_group = operands
        scores = jnp.einsum('tgd,pd->gtp', query_group.astype(jnp.float32), key_group.astype(jnp.float32)) * score_scale
        scores = jnp.where(allowed[None], scores, -jnp.inf)
        row_max = lax.optimization_barrier(jnp.max(scores, axis=-1, keepdims=True))
        weights = jnp.where(allowed[None], jnp.exp(scores - row_max), 0.0)
        weight_sum = lax.optimization_barrier(jnp.sum(weights, axis=-1))
        rounded = lax.optimization_barrier(weights.astype(jnp.bfloat16)).astype(jnp.float32)
        blended = jnp.einsum('gtp,pd->tgd', rounded, value_group.astype(jnp.float32))
        return blended / jnp.transpose(weight_sum)[:, :, None]
    per_group = lax.map(one_group, (grouped, cache_keys, cache_values))
    return jnp.transpose(per_group, (1, 0, 2, 3)).reshape(NEW, QH * HD)

def reference(queries, kv_cache, start_positions, residual, out_weight, norm_gain, gate_weight, up_weight, down_weight):
    pieces = []
    for sequence in range(SEQS):
        query_rows = queries[sequence * NEW:(sequence + 1) * NEW]
        cache_keys = kv_cache[0, sequence].reshape(KVH, CACHE, HD)
        cache_values = kv_cache[1, sequence].reshape(KVH, CACHE, HD)
        last_valid = start_positions[sequence] + jnp.arange(NEW, dtype=jnp.int32)
        pieces.append(attend_sequence(query_rows, cache_keys, cache_values, last_valid))
    attended = jnp.concatenate(pieces, 0).astype(jnp.bfloat16)
    projected = jnp.dot(attended, out_weight, preferred_element_type=jnp.float32)
    resid = (residual.astype(jnp.float32) + projected).astype(jnp.bfloat16)
    resid_wide = resid.astype(jnp.float32)
    square = lax.optimization_barrier(jnp.sum(resid_wide * resid_wide, axis=1, keepdims=True))
    scaled = (resid_wide * norm_gain.astype(jnp.float32)).astype(jnp.bfloat16)
    inverse = lax.rsqrt(square / D + 1e-05)
    gate = jnp.dot(scaled, gate_weight, preferred_element_type=jnp.float32) * inverse
    up_part = jnp.dot(scaled, up_weight, preferred_element_type=jnp.float32) * inverse
    hidden = (jax.nn.silu(gate) * up_part).astype(jnp.bfloat16)
    down_part = jnp.dot(hidden, down_weight, preferred_element_type=jnp.float32)
    return (resid_wide + down_part).astype(jnp.bfloat16)
```

```python
import math

import jax
import jax.numpy as jnp
import jax.experimental.pallas as pl
import jax.experimental.pallas.tpu as pltpu
from jax import lax
from jax.sharding import PartitionSpec as P

D = 8192
QH = 64
KVH = 8
HD = 128


NEG_FILL = -1e30
EPSILON = 1e-05
MESH = pl.DeviceIdType.MESH


def merged(value, axis, join):
    pieces = jax.tree.map(lambda part: lax.all_gather(part, axis), value)
    head = jax.tree.map(lambda part: part[0], pieces)
    tail = jax.tree.map(lambda part: part[1:], pieces)
    so_far, _ = lax.scan(lambda so_far, section: (join(so_far, section), None), head, tail)
    return so_far


def block_scores(query_block, cache_keys, cache_values, start_positions, first_position):
    new_count = query_block.shape[0] // cache_keys.shape[0]
    score_scale = 1.0 / math.sqrt(cache_keys.shape[2])
    positions = first_position + jnp.arange(cache_keys.shape[1], dtype=jnp.int32)
    maxima = []
    totals = []
    blends = []
    for sequence in range(cache_keys.shape[0]):
        rows_here = query_block[sequence * new_count : (sequence + 1) * new_count]
        scores = (
            jnp.einsum(
                "tkd,pd->ktp", rows_here, cache_keys[sequence], preferred_element_type=jnp.float32
            )
            * score_scale
        )
        last_valid = start_positions[sequence] + jnp.arange(new_count, dtype=jnp.int32)
        allowed = (positions[None, :] <= last_valid[:, None])[None]
        scores = jnp.where(allowed, scores, NEG_FILL)
        row_max = jnp.max(scores, axis=-1)
        weights = jnp.where(allowed, jnp.exp(scores - row_max[..., None]), 0.0)
        maxima.append(jnp.transpose(row_max))
        totals.append(jnp.transpose(jnp.sum(weights, axis=-1)))
        blends.append(
            jnp.einsum(
                "ktp,pd->tkd",
                weights.astype(jnp.bfloat16),
                cache_values[sequence],
                preferred_element_type=jnp.float32,
            )
        )
    return (jnp.concatenate(maxima, 0), jnp.concatenate(totals, 0), jnp.concatenate(blends, 0))


def merge_parts(earlier, later):
    joint = jnp.maximum(earlier[0], later[0])
    early_scale = jnp.exp(earlier[0] - joint)
    late_scale = jnp.exp(later[0] - joint)
    return (
        joint,
        earlier[1] * early_scale + later[1] * late_scale,
        earlier[2] * early_scale[..., None] + later[2] * late_scale[..., None],
    )


def local(
    queries,
    kv_cache,
    start_positions,
    residual,
    out_weight,
    norm_gain,
    gate_weight,
    up_weight,
    down_weight,
):
    head_count = lax.axis_size("heads")
    row_count = lax.axis_size("rows")
    head_index = lax.axis_index("heads")
    row_index = lax.axis_index("rows")
    row_block = queries.shape[0]
    total_rows = row_block * head_count
    group_size = QH // KVH
    per_group = head_count * row_count // KVH
    pos_count = kv_cache.shape[2]
    own_shard = head_index * row_count + row_index
    first_position = own_shard % per_group * pos_count
    shard_ids = jnp.arange(head_count, dtype=jnp.int32) * row_count + row_index
    shard_groups = shard_ids // per_group
    grouped = queries.reshape(row_block, KVH, group_size, HD)
    outgoing = jnp.stack(
        [
            lax.dynamic_index_in_dim(
                grouped, (i * row_count + row_index) // per_group, 1, keepdims=False
            )
            for i in range(head_count)
        ],
        axis=1,
    )
    row_max, weight_sum, blended = block_scores(
        lax.all_to_all(outgoing, "heads", split_axis=1, concat_axis=0, tiled=True)[:, 0],
        kv_cache[0],
        kv_cache[1],
        start_positions,
        first_position,
    )
    got_max, got_sum, got_blend = (
        lax.all_to_all(
            row_max.reshape(head_count, row_block, group_size),
            "heads",
            split_axis=0,
            concat_axis=0,
            tiled=True,
        ),
        lax.all_to_all(
            weight_sum.reshape(head_count, row_block, group_size),
            "heads",
            split_axis=0,
            concat_axis=0,
            tiled=True,
        ),
        lax.all_to_all(
            blended.reshape(head_count, row_block, group_size, HD),
            "heads",
            split_axis=0,
            concat_axis=0,
            tiled=True,
        ),
    )
    member = (shard_groups[:, None] == jnp.arange(KVH, dtype=jnp.int32)[None, :])[:, None, :, None]
    spread_max = jnp.where(member, got_max[:, :, None, :], NEG_FILL)
    canvas_max = jnp.max(spread_max, axis=0)
    factor = jnp.where(member, jnp.exp(got_max[:, :, None, :] - canvas_max[None]), 0.0)
    canvas_sum = jnp.sum(factor * got_sum[:, :, None, :], axis=0)
    canvas_blend = jnp.einsum("srkg,srgd->rkgd", factor, got_blend, precision=lax.Precision.HIGHEST)
    joint_max, joint_sum, joint_blend = merged(
        (canvas_max, canvas_sum, canvas_blend), "rows", merge_parts
    )
    attended = (
        (joint_blend / joint_sum[..., None]).reshape(row_block, head_count, -1).astype(jnp.bfloat16)
    )
    head_rows = lax.all_to_all(attended, "heads", split_axis=1, concat_axis=0, tiled=True).reshape(
        total_rows, -1
    )
    row_start = head_index * row_block
    local_term = jnp.dot(head_rows, out_weight, preferred_element_type=jnp.float32)
    own_rows = lax.dynamic_slice_in_dim(local_term, row_start, row_block, 0) + residual.astype(
        jnp.float32
    )
    local_term = lax.dynamic_update_slice_in_dim(local_term, own_rows, row_start, 0)
    resid_all = lax.psum(local_term, "heads").astype(jnp.bfloat16)
    resid_own = lax.dynamic_slice_in_dim(resid_all, row_start, row_block, 0)
    resid_wide = resid_all.astype(jnp.float32)
    square = jnp.sum(resid_wide * resid_wide, axis=1)
    scaled = (resid_wide * norm_gain).astype(jnp.bfloat16)
    gate_part = jnp.dot(scaled, gate_weight, preferred_element_type=jnp.float32)
    up_part = jnp.dot(scaled, up_weight, preferred_element_type=jnp.float32)
    gate_sum, up_sum, square_sum = lax.psum((gate_part, up_part, square), "rows")
    inverse = lax.rsqrt(square_sum / D + EPSILON)[:, None]
    hidden = (jax.nn.silu(gate_sum * inverse) * (up_sum * inverse)).astype(jnp.bfloat16)
    down_sum = lax.psum_scatter(
        jnp.dot(hidden, down_weight, preferred_element_type=jnp.float32),
        "heads",
        scatter_dimension=0,
        tiled=True,
    )
    return (resid_own.astype(jnp.float32) + down_sum).astype(jnp.bfloat16)


def fused_kernel(
    q_hbm, kv_hbm, start_ref, res_hbm, wo_hbm, gain_ref, wg_hbm, wu_hbm, wd_hbm, out_ref,
    wo, wg, wu, wd2, qbuf, kvbuf, attn, zsend, zrecv, resid, res, scl, gsend, grecv,
    xrecv, hid, sqs, sqr, sqx,
    lsem, qss, qrs, kss, krs, asx, arx, asc, arc, asf, arf, zss, zrs, rss, rrs, gss, grs,
    xss, xrs, sss, srs, hsx, hrx, hsc, hrc, hsf, hrf, dss, drs,
):
    h = lax.axis_index("heads")
    r = lax.axis_index("rows")
    x = r // 2
    c = r % 2
    core_peer = x * 2 + (1 - c)
    chip_peer = (1 - x) * 2 + c
    block = zrecv.shape[2]
    span = 4 * block
    pair = 2 * block
    width = qbuf.shape[2]
    depth = wo.shape[1]
    quarter = hid.shape[2] // 4
    first = wo.shape[0]

    def remote(src, dst, ss, rs, hh, rr):
        return pltpu.make_async_remote_copy(
            src_ref=src, dst_ref=dst, send_sem=ss, recv_sem=rs,
            device_id={"heads": hh, "rows": rr}, device_id_type=MESH,
        )

    def lanes(start, size):
        return pl.ds(pl.multiple_of(start, 128), size)

    def subl(start, size):
        return pl.ds(pl.multiple_of(start, 32), size)

    def ring(d):
        return lax.rem(h + d, 4)

    kv_own = pltpu.make_async_copy(kv_hbm.at[:, c], kvbuf.at[:, c], lsem.at[0])
    kv_own.start()
    q_own = pltpu.make_async_copy(
        q_hbm.at[:, :, lanes((2 * h + x) * width, width)],
        qbuf.at[:, subl(lax.rem(h, 2) * block, block), :],
        lsem.at[1],
    )
    sender = c == h // 2

    @pl.when(sender)
    def _():
        q_own.start()

    barrier = pltpu.get_barrier_semaphore()
    for d in (1, 2, 3):
        pl.semaphore_signal(
            barrier, inc=1, device_id={"heads": ring(d), "rows": r}, device_id_type=MESH
        )
        pl.semaphore_signal(
            barrier, inc=1, device_id={"heads": h, "rows": lax.rem(r + d, 4)}, device_id_type=MESH
        )
    pl.semaphore_wait(barrier, 6)

    def q_copy(d):
        hh = ring(d)
        return remote(
            q_hbm.at[:, :, lanes((2 * hh + x) * width, width)],
            qbuf.at[:, subl(lax.rem(h, 2) * block, block), :],
            qss.at[d - 1], qrs.at[lax.rem(h, 2)], hh, r,
        )

    @pl.when(sender)
    def _():
        for d in (2, 1, 3):
            q_copy(d).start()

    kv_copy = remote(kv_hbm.at[:, 1 - c], kvbuf.at[:, c], kss.at[0], krs.at[0], h, core_peer)
    kv_copy.start()

    res_load = pltpu.make_async_copy(res_hbm, res, lsem.at[2])
    wo_load = pltpu.make_async_copy(wo_hbm, wo, lsem.at[3])
    wg_load = pltpu.make_async_copy(wg_hbm, wg, lsem.at[4])
    wu_load = pltpu.make_async_copy(wu_hbm, wu, lsem.at[5])
    wd2_load = pltpu.make_async_copy(
        wd_hbm.at[pl.ds(first, wd2.shape[0]), :], wd2, lsem.at[6]
    )
    wd1_load = pltpu.make_async_copy(wd_hbm.at[pl.ds(0, first), :], wo, lsem.at[7])
    for load in (res_load, wo_load, wg_load, wu_load, wd2_load):
        load.start()

    kv_own.wait()
    remote(
        kv_hbm.at[:, 1 - c], kvbuf.at[:, 1 - c], kss.at[0], krs.at[0], h, core_peer
    ).wait_recv()
    for j in (0, 1):
        here = sender & (lax.rem(h, 2) == j)

        @pl.when(here)
        def _():
            q_own.wait()

        @pl.when(jnp.logical_not(here))
        def _():
            remote(
                q_hbm.at[:, :, pl.ds(0, width)], qbuf.at[:, pl.ds(j * block, block), :],
                qss.at[0], qrs.at[j], ring(1), r,
            ).wait_recv()

    scale = 1.0 / math.sqrt(HD)
    start = start_ref[c]
    positions = kvbuf.shape[1] * kvbuf.shape[2]

    def head_body(k, half):
        row = lax.broadcasted_iota(jnp.int32, (pair, 1), 0)
        token = (row // block) * pair + half * block + row % block
        col = lax.broadcasted_iota(jnp.int32, (pair, positions), 1)
        allowed = col <= start + token
        s = lax.dot_general(
            qbuf[half, :, lanes(k * HD, HD)], kvbuf[0].reshape(positions, HD),
            (((1,), (1,)), ((), ())), preferred_element_type=jnp.float32,
        ) * scale
        s = jnp.where(allowed, s, NEG_FILL)
        p = jnp.exp(s - jnp.max(s, axis=1, keepdims=True))
        total = jnp.sum(p, axis=1, keepdims=True)
        o = jnp.dot(
            p.astype(jnp.bfloat16), kvbuf[1].reshape(positions, HD),
            preferred_element_type=jnp.float32,
        )
        attn[half, subl(c * pair, pair), lanes(x * width + k * HD, HD)] = (o / total).astype(
            jnp.bfloat16
        )

    piece = width // 4

    def attn_block(cc, xx, ch):
        return attn.at[:, subl(cc * pair, pair), lanes(xx * width + ch * piece, piece)]

    def attn_body(ch, carry):
        for k in range(piece // HD):
            for half in (0, 1):
                head_body(ch * (piece // HD) + k, half)
        mine = attn_block(c, x, ch)
        remote(mine, mine, asx.at[ch], arx.at[ch], h, chip_peer).start()
        remote(mine, mine, asc.at[ch], arc.at[ch], h, core_peer).start()
        return carry

    lax.fori_loop(0, 4, attn_body, 0)

    def forward_body(ch, carry):
        far = attn_block(c, 1 - x, ch)
        remote(far, far, asx.at[ch], arx.at[ch], h, chip_peer).wait_recv()
        remote(far, far, asf.at[ch], arf.at[ch], h, core_peer).start()
        return carry

    lax.fori_loop(0, 4, forward_body, 0)

    def gathered_body(ch, carry):
        near = attn_block(1 - c, x, ch)
        far = attn_block(1 - c, 1 - x, ch)
        remote(near, near, asc.at[ch], arc.at[ch], h, core_peer).wait_recv()
        remote(far, far, asf.at[ch], arf.at[ch], h, core_peer).wait_recv()
        mine = attn_block(c, x, ch)
        remote(mine, mine, asx.at[ch], arx.at[ch], h, chip_peer).wait_send()
        remote(mine, mine, asc.at[ch], arc.at[ch], h, core_peer).wait_send()
        remote(mine, mine, asf.at[ch], arf.at[ch], h, core_peer).wait_send()
        return carry

    lax.fori_loop(0, 4, gathered_body, 0)
    wo_load.wait()
    res_load.wait()
    cols = 512

    def z_copy(half, d, target, ss, rs):
        hh = ring(d)
        return remote(
            zsend.at[half, subl(hh * block, block), :], target.at[half, d - 1],
            ss.at[half, d - 1], rs.at[half, d - 1], hh, r,
        )

    def project_body(half, carry):
        def chunk(n, inner):
            part = jnp.dot(
                attn[half], wo[:, lanes(n * cols, cols)], preferred_element_type=jnp.float32
            )
            zsend[half, :, lanes(n * cols, cols)] = part.astype(jnp.bfloat16)
            return inner

        lax.fori_loop(0, depth // cols, chunk, 0)
        for d in (2, 1, 3):
            z_copy(half, d, zrecv, zss, zrs).start()
        return carry

    lax.fori_loop(0, 2, project_body, 0)
    wd1_load.start()

    def r_copy(half, d, source):
        mine = resid.at[half, subl(source * block, block), :]
        return remote(mine, mine, rss.at[half, d - 1], rrs.at[half, d - 1], ring(d), r)

    def resid_body(half, carry):
        for d in (1, 2, 3):
            z_copy(half, d, zrecv, zss, zrs).wait_recv()
        total = zsend[half, subl(h * block, block), :].astype(jnp.float32)
        for d in (1, 2, 3):
            total = total + zrecv[half, d - 1].astype(jnp.float32)
        total = total + res[half].astype(jnp.float32)
        resid[half, subl(h * block, block), :] = total.astype(jnp.bfloat16)
        for d in (2, 1, 3):
            r_copy(half, d, h).start()
        return carry

    lax.fori_loop(0, 2, resid_body, 0)
    wg_load.wait()
    wu_load.wait()

    def both(qi):
        at = lanes(qi * quarter, quarter)
        return (
            jnp.dot(scl[...], wg[:, at], preferred_element_type=jnp.float32),
            jnp.dot(scl[...], wu[:, at], preferred_element_type=jnp.float32),
        )

    def g_copy(half, xx):
        return remote(
            gsend.at[xx], grecv.at[half, xx], gss.at[half, xx], grs.at[half, xx], h, core_peer
        )

    def sq_copy(half):
        return remote(sqs.at[half], sqr.at[half], sss.at[half, 0], srs.at[half, 0], h, core_peer)

    def sq_copy2(half):
        return remote(sqr.at[half], sqx.at[half], sss.at[half, 1], srs.at[half, 1], h, chip_peer)

    def x_copy(half):
        return remote(grecv.at[half, 1 - x], xrecv.at[half], xss.at[half], xrs.at[half], h, chip_peer)

    def gate_body(half, carry):
        for d in (1, 2, 3):
            r_copy(half, d, lax.rem(h + 4 - d, 4)).wait_recv()
        wide = resid[half].astype(jnp.float32)
        sqs[half] = jnp.broadcast_to(jnp.sum(wide * wide, axis=1, keepdims=True), (span, 128))
        sq_copy(half).start()
        scl[...] = (wide * gain_ref[...]).astype(jnp.bfloat16)

        @pl.when(half == 1)
        def _():
            for xx in (0, 1):
                g_copy(0, xx).wait_send()

        def partner(i, inner):
            xx = lax.rem(1 - x + i, 2)
            g, u = both(2 * xx + 1 - c)
            gsend[xx, :, 0:quarter] = g.astype(jnp.bfloat16)
            gsend[xx, :, quarter:] = u.astype(jnp.bfloat16)
            g_copy(half, xx).start()
            return inner

        lax.fori_loop(0, 2, partner, 0)
        g, u = both(2 * (1 - x) + c)
        g_copy(half, 1 - x).wait_recv()
        grecv[half, 1 - x, :, 0:quarter] = (
            g + grecv[half, 1 - x, :, 0:quarter].astype(jnp.float32)
        ).astype(jnp.bfloat16)
        grecv[half, 1 - x, :, quarter:] = (
            u + grecv[half, 1 - x, :, quarter:].astype(jnp.float32)
        ).astype(jnp.bfloat16)
        x_copy(half).start()
        sq_copy(half).wait_recv()
        sqr[half] = sqs[half] + sqr[half]
        sq_copy2(half).start()
        g, u = both(2 * x + c)
        g_copy(half, x).wait_recv()
        grecv[half, x, :, 0:quarter] = (
            g + grecv[half, x, :, 0:quarter].astype(jnp.float32)
        ).astype(jnp.bfloat16)
        grecv[half, x, :, quarter:] = (
            u + grecv[half, x, :, quarter:].astype(jnp.float32)
        ).astype(jnp.bfloat16)
        return carry

    lax.fori_loop(0, 2, gate_body, 0)

    def h_copy(half, owner, ss, rs, rr):
        mine = hid.at[half, :, lanes(owner * quarter, quarter)]
        return remote(mine, mine, ss.at[half], rs.at[half], h, rr)

    def hidden_body(half, carry):
        x_copy(half).wait_recv()
        sq_copy2(half).wait_recv()
        square = (sqr[half] + sqx[half])[:, 0:1]
        inverse = lax.rsqrt(square / D + EPSILON)
        summed = grecv[half, x].astype(jnp.float32) + xrecv[half].astype(jnp.float32)
        gate = summed[:, 0:quarter] * inverse
        up = summed[:, quarter:] * inverse
        hid[half, :, lanes(r * quarter, quarter)] = (gate / (1.0 + jnp.exp(-gate)) * up).astype(
            jnp.bfloat16
        )
        h_copy(half, r, hsx, hrx, chip_peer).start()
        h_copy(half, r, hsc, hrc, core_peer).start()
        return carry

    lax.fori_loop(0, 2, hidden_body, 0)
    wd1_load.wait()
    wd2_load.wait()

    def down_body(half, carry):
        h_copy(half, chip_peer, hsx, hrx, chip_peer).wait_recv()
        h_copy(half, chip_peer, hsf, hrf, core_peer).start()
        for d in (1, 2, 3):
            z_copy(half, d, zrecv, zss, zrs).wait_send()
        h_copy(half, core_peer, hsc, hrc, core_peer).wait_recv()
        h_copy(half, 2 * (1 - x) + 1 - c, hsf, hrf, core_peer).wait_recv()

        def chunk(n, inner):
            at = lanes(n * cols, cols)
            part = jnp.dot(
                hid[half, :, 0:first], wo[:, at], preferred_element_type=jnp.float32
            ) + jnp.dot(hid[half, :, first:], wd2[:, at], preferred_element_type=jnp.float32)
            zsend[half, :, at] = part.astype(jnp.bfloat16)
            return inner

        lax.fori_loop(0, depth // cols, chunk, 0)
        for d in (2, 1, 3):
            z_copy(half, d, zrecv, dss, drs).start()
        return carry

    lax.fori_loop(0, 2, down_body, 0)

    def final_body(half, carry):
        for d in (1, 2, 3):
            z_copy(half, d, zrecv, dss, drs).wait_recv()
        total = zsend[half, subl(h * block, block), :].astype(jnp.float32)
        for d in (1, 2, 3):
            total = total + zrecv[half, d - 1].astype(jnp.float32)
        total = total + resid[half, subl(h * block, block), :].astype(jnp.float32)
        out_ref[half] = total.astype(jnp.bfloat16)
        return carry

    lax.fori_loop(0, 2, final_body, 0)

    @pl.when(sender)
    def _():
        for d in (1, 2, 3):
            q_copy(d).wait_send()

    kv_copy.wait_send()

    def drain(half, carry):
        for d in (1, 2, 3):
            r_copy(half, d, h).wait_send()
            z_copy(half, d, zrecv, dss, drs).wait_send()
        sq_copy(half).wait_send()
        sq_copy2(half).wait_send()
        x_copy(half).wait_send()
        h_copy(half, r, hsx, hrx, chip_peer).wait_send()
        h_copy(half, r, hsc, hrc, core_peer).wait_send()
        h_copy(half, chip_peer, hsf, hrf, core_peer).wait_send()
        return carry

    lax.fori_loop(0, 2, drain, 0)
    for xx in (0, 1):
        g_copy(1, xx).wait_send()


def fused(
    queries, kv_cache, start_positions, residual, out_weight, norm_gain, gate_weight, up_weight,
    down_weight,
):
    rows, wide = queries.shape
    block = rows // 2
    span = 4 * block
    width = wide // KVH
    depth = residual.shape[1]
    units = gate_weight.shape[1]
    quarter = units // 4
    first = out_weight.shape[0]
    half_rest = units - first
    bf, f32 = jnp.bfloat16, jnp.float32
    vmem, dma = pltpu.VMEM, pltpu.SemaphoreType.DMA
    anyspace = pl.BlockSpec(memory_space=pl.ANY)
    vspec = pl.BlockSpec(memory_space=pltpu.VMEM)
    out = pl.pallas_call(
        fused_kernel,
        out_shape=jax.ShapeDtypeStruct((2, block, depth), bf),
        in_specs=[
            anyspace, anyspace, pl.BlockSpec(memory_space=pltpu.SMEM), anyspace, anyspace, vspec,
            anyspace, anyspace, anyspace,
        ],
        out_specs=vspec,
        scratch_shapes=[
            vmem((first, depth), bf),
            vmem((depth, units), bf),
            vmem((depth, units), bf),
            vmem((half_rest, depth), bf),
            vmem((2, 2 * block, width), bf),
            vmem(kv_cache.shape, bf),
            vmem((2, span, 2 * width), bf),
            vmem((2, span, depth), bf),
            vmem((2, 3, block, depth), bf),
            vmem((2, span, depth), bf),
            vmem((2, block, depth), bf),
            vmem((span, depth), bf),
            vmem((2, span, 2 * quarter), bf),
            vmem((2, 2, span, 2 * quarter), bf),
            vmem((2, span, 2 * quarter), bf),
            vmem((2, span, units), bf),
            vmem((2, span, 128), f32),
            vmem((2, span, 128), f32),
            vmem((2, span, 128), f32),
            dma((8,)), dma((3,)), dma((2,)), dma((1,)), dma((1,)),
            dma((4,)), dma((4,)), dma((4,)), dma((4,)), dma((4,)), dma((4,)),
            dma((2, 3)), dma((2, 3)), dma((2, 3)), dma((2, 3)),
            dma((2, 2)), dma((2, 2)), dma((2,)), dma((2,)), dma((2, 2)), dma((2, 2)),
            dma((2,)), dma((2,)), dma((2,)), dma((2,)), dma((2,)), dma((2,)),
            dma((2, 3)), dma((2, 3)),
        ],
        compiler_params=pltpu.CompilerParams(
            collective_id=0, has_side_effects=True, vmem_limit_bytes=63 * 1024 * 1024
        ),
    )(
        queries.reshape(2, block, wide), kv_cache, start_positions,
        residual.reshape(2, block, depth), out_weight, norm_gain.reshape(1, depth), gate_weight,
        up_weight, down_weight,
    )
    return out.reshape(rows, depth)


def one_kernel_fits(mesh):
    return mesh.shape["heads"] == 4 and mesh.shape["rows"] == 4


def solution(mesh):
    return jax.shard_map(
        fused if one_kernel_fits(mesh) else local,
        mesh=mesh,
        in_specs=(
            P(("groups", "heads"), None),
            P(None, "groups", ("heads", "rows"), None),
            P("groups"),
            P(("groups", "heads"), "rows"),
            P("heads", "rows"),
            P("rows"),
            P("rows", "heads"),
            P("rows", "heads"),
            P("heads", "rows"),
        ),
        out_specs=P(("groups", "heads"), "rows"),
        check_vma=False,
    )
```

```python
import math

import jax
import jax.numpy as jnp
import jax.experimental.pallas as pl
import jax.experimental.pallas.tpu as pltpu
from jax import lax
from jax.sharding import PartitionSpec as P

D = 8192
QH = 64
KVH = 8
HD = 128


NEG_FILL = -1e30
EPSILON = 1e-05
MESH = pl.DeviceIdType.MESH


def merged(value, axis, join):
    pieces = jax.tree.map(lambda part: lax.all_gather(part, axis), value)
    head = jax.tree.map(lambda part: part[0], pieces)
    tail = jax.tree.map(lambda part: part[1:], pieces)
    so_far, _ = lax.scan(lambda so_far, section: (join(so_far, section), None), head, tail)
    return so_far


def block_scores(query_block, cache_keys, cache_values, start_positions, first_position):
    new_count = query_block.shape[0] // cache_keys.shape[0]
    score_scale = 1.0 / math.sqrt(cache_keys.shape[2])
    positions = first_position + jnp.arange(cache_keys.shape[1], dtype=jnp.int32)
    maxima = []
    totals = []
    blends = []
    for sequence in range(cache_keys.shape[0]):
        rows_here = query_block[sequence * new_count : (sequence + 1) * new_count]
        scores = (
            jnp.einsum(
                "tkd,pd->ktp", rows_here, cache_keys[sequence], preferred_element_type=jnp.float32
            )
            * score_scale
        )
        last_valid = start_positions[sequence] + jnp.arange(new_count, dtype=jnp.int32)
        allowed = (positions[None, :] <= last_valid[:, None])[None]
        scores = jnp.where(allowed, scores, NEG_FILL)
        row_max = jnp.max(scores, axis=-1)
        weights = jnp.where(allowed, jnp.exp(scores - row_max[..., None]), 0.0)
        maxima.append(jnp.transpose(row_max))
        totals.append(jnp.transpose(jnp.sum(weights, axis=-1)))
        blends.append(
            jnp.einsum(
                "ktp,pd->tkd",
                weights.astype(jnp.bfloat16),
                cache_values[sequence],
                preferred_element_type=jnp.float32,
            )
        )
    return (jnp.concatenate(maxima, 0), jnp.concatenate(totals, 0), jnp.concatenate(blends, 0))


def merge_parts(earlier, later):
    joint = jnp.maximum(earlier[0], later[0])
    early_scale = jnp.exp(earlier[0] - joint)
    late_scale = jnp.exp(later[0] - joint)
    return (
        joint,
        earlier[1] * early_scale + later[1] * late_scale,
        earlier[2] * early_scale[..., None] + later[2] * late_scale[..., None],
    )


def local(
    queries,
    kv_cache,
    start_positions,
    residual,
    out_weight,
    norm_gain,
    gate_weight,
    up_weight,
    down_weight,
):
    head_count = lax.axis_size("heads")
    row_count = lax.axis_size("rows")
    head_index = lax.axis_index("heads")
    row_index = lax.axis_index("rows")
    row_block = queries.shape[0]
    total_rows = row_block * head_count
    group_size = QH // KVH
    per_group = head_count * row_count // KVH
    pos_count = kv_cache.shape[2]
    own_shard = head_index * row_count + row_index
    first_position = own_shard % per_group * pos_count
    shard_ids = jnp.arange(head_count, dtype=jnp.int32) * row_count + row_index
    shard_groups = shard_ids // per_group
    grouped = queries.reshape(row_block, KVH, group_size, HD)
    outgoing = jnp.stack(
        [
            lax.dynamic_index_in_dim(
                grouped, (i * row_count + row_index) // per_group, 1, keepdims=False
            )
            for i in range(head_count)
        ],
        axis=1,
    )
    row_max, weight_sum, blended = block_scores(
        lax.all_to_all(outgoing, "heads", split_axis=1, concat_axis=0, tiled=True)[:, 0],
        kv_cache[0],
        kv_cache[1],
        start_positions,
        first_position,
    )
    got_max, got_sum, got_blend = (
        lax.all_to_all(
            row_max.reshape(head_count, row_block, group_size),
            "heads",
            split_axis=0,
            concat_axis=0,
            tiled=True,
        ),
        lax.all_to_all(
            weight_sum.reshape(head_count, row_block, group_size),
            "heads",
            split_axis=0,
            concat_axis=0,
            tiled=True,
        ),
        lax.all_to_all(
            blended.reshape(head_count, row_block, group_size, HD),
            "heads",
            split_axis=0,
            concat_axis=0,
            tiled=True,
        ),
    )
    member = (shard_groups[:, None] == jnp.arange(KVH, dtype=jnp.int32)[None, :])[:, None, :, None]
    spread_max = jnp.where(member, got_max[:, :, None, :], NEG_FILL)
    canvas_max = jnp.max(spread_max, axis=0)
    factor = jnp.where(member, jnp.exp(got_max[:, :, None, :] - canvas_max[None]), 0.0)
    canvas_sum = jnp.sum(factor * got_sum[:, :, None, :], axis=0)
    canvas_blend = jnp.einsum("srkg,srgd->rkgd", factor, got_blend, precision=lax.Precision.HIGHEST)
    joint_max, joint_sum, joint_blend = merged(
        (canvas_max, canvas_sum, canvas_blend), "rows", merge_parts
    )
    attended = (
        (joint_blend / joint_sum[..., None]).reshape(row_block, head_count, -1).astype(jnp.bfloat16)
    )
    head_rows = lax.all_to_all(attended, "heads", split_axis=1, concat_axis=0, tiled=True).reshape(
        total_rows, -1
    )
    row_start = head_index * row_block
    local_term = jnp.dot(head_rows, out_weight, preferred_element_type=jnp.float32)
    own_rows = lax.dynamic_slice_in_dim(local_term, row_start, row_block, 0) + residual.astype(
        jnp.float32
    )
    local_term = lax.dynamic_update_slice_in_dim(local_term, own_rows, row_start, 0)
    resid_all = lax.psum(local_term, "heads").astype(jnp.bfloat16)
    resid_own = lax.dynamic_slice_in_dim(resid_all, row_start, row_block, 0)
    resid_wide = resid_all.astype(jnp.float32)
    square = jnp.sum(resid_wide * resid_wide, axis=1)
    scaled = (resid_wide * norm_gain).astype(jnp.bfloat16)
    gate_part = jnp.dot(scaled, gate_weight, preferred_element_type=jnp.float32)
    up_part = jnp.dot(scaled, up_weight, preferred_element_type=jnp.float32)
    gate_sum, up_sum, square_sum = lax.psum((gate_part, up_part, square), "rows")
    inverse = lax.rsqrt(square_sum / D + EPSILON)[:, None]
    hidden = (jax.nn.silu(gate_sum * inverse) * (up_sum * inverse)).astype(jnp.bfloat16)
    down_sum = lax.psum_scatter(
        jnp.dot(hidden, down_weight, preferred_element_type=jnp.float32),
        "heads",
        scatter_dimension=0,
        tiled=True,
    )
    return (resid_own.astype(jnp.float32) + down_sum).astype(jnp.bfloat16)


def fused_kernel(
    q_hbm, kv_hbm, start_ref, res_hbm, wo_hbm, gain_ref, wg_hbm, wu_hbm, wd_hbm, out_ref,
    wo, wg, wu, wd2, qbuf, kvbuf, attn, zsend, zrecv, resid, res, scl, gsend, grecv,
    xrecv, hid, sqs, sqr, sqx,
    lsem, qss, qrs, kss, krs, asx, arx, asc, arc, asf, arf, zss, zrs, rss, rrs, gss, grs,
    xss, xrs, sss, srs, hsx, hrx, hsc, hrc, hsf, hrf, dss, drs,
):
    h = lax.axis_index("heads")
    r = lax.axis_index("rows")
    x = r // 2
    c = r % 2
    core_peer = x * 2 + (1 - c)
    chip_peer = (1 - x) * 2 + c
    block = zrecv.shape[2]
    span = 4 * block
    pair = 2 * block
    width = qbuf.shape[2]
    depth = wo.shape[1]
    quarter = hid.shape[2] // 4
    first = wo.shape[0]

    def remote(src, dst, ss, rs, hh, rr):
        return pltpu.make_async_remote_copy(
            src_ref=src, dst_ref=dst, send_sem=ss, recv_sem=rs,
            device_id={"heads": hh, "rows": rr}, device_id_type=MESH,
        )

    def lanes(start, size):
        return pl.ds(pl.multiple_of(start, 128), size)

    def subl(start, size):
        return pl.ds(pl.multiple_of(start, 32), size)

    def ring(d):
        return lax.rem(h + d, 4)

    kv_own = pltpu.make_async_copy(kv_hbm.at[:, c], kvbuf.at[:, c], lsem.at[0])
    kv_own.start()
    q_own = pltpu.make_async_copy(
        q_hbm.at[:, :, lanes((2 * h + x) * width, width)],
        qbuf.at[:, subl(lax.rem(h, 2) * block, block), :],
        lsem.at[1],
    )
    sender = c == h // 2

    @pl.when(sender)
    def _():
        q_own.start()

    barrier = pltpu.get_barrier_semaphore()
    for d in (1, 2, 3):
        pl.semaphore_signal(
            barrier, inc=1, device_id={"heads": ring(d), "rows": r}, device_id_type=MESH
        )
        pl.semaphore_signal(
            barrier, inc=1, device_id={"heads": h, "rows": lax.rem(r + d, 4)}, device_id_type=MESH
        )
    pl.semaphore_wait(barrier, 6)

    def q_copy(d):
        hh = ring(d)
        return remote(
            q_hbm.at[:, :, lanes((2 * hh + x) * width, width)],
            qbuf.at[:, subl(lax.rem(h, 2) * block, block), :],
            qss.at[d - 1], qrs.at[lax.rem(h, 2)], hh, r,
        )

    @pl.when(sender)
    def _():
        for d in (2, 1, 3):
            q_copy(d).start()

    kv_copy = remote(kv_hbm.at[:, 1 - c], kvbuf.at[:, c], kss.at[0], krs.at[0], h, core_peer)
    kv_copy.start()

    res_load = pltpu.make_async_copy(res_hbm, res, lsem.at[2])
    wo_load = pltpu.make_async_copy(wo_hbm, wo, lsem.at[3])
    wg_load = pltpu.make_async_copy(wg_hbm, wg, lsem.at[4])
    wu_load = pltpu.make_async_copy(wu_hbm, wu, lsem.at[5])
    wd2_load = pltpu.make_async_copy(
        wd_hbm.at[pl.ds(first, wd2.shape[0]), :], wd2, lsem.at[6]
    )
    wd1_load = pltpu.make_async_copy(wd_hbm.at[pl.ds(0, first), :], wo, lsem.at[7])
    for load in (res_load, wo_load, wg_load, wu_load, wd2_load):
        load.start()

    kv_own.wait()
    remote(
        kv_hbm.at[:, 1 - c], kvbuf.at[:, 1 - c], kss.at[0], krs.at[0], h, core_peer
    ).wait_recv()
    for j in (0, 1):
        here = sender & (lax.rem(h, 2) == j)

        @pl.when(here)
        def _():
            q_own.wait()

        @pl.when(jnp.logical_not(here))
        def _():
            remote(
                q_hbm.at[:, :, pl.ds(0, width)], qbuf.at[:, pl.ds(j * block, block), :],
                qss.at[0], qrs.at[j], ring(1), r,
            ).wait_recv()

    scale = 1.0 / math.sqrt(HD)
    start = start_ref[c]
    positions = kvbuf.shape[1] * kvbuf.shape[2]

    def head_body(k):
        row = lax.broadcasted_iota(jnp.int32, (span, 1), 0)
        token = (row % pair // block) * pair + row // pair * block + row % block
        col = lax.broadcasted_iota(jnp.int32, (span, positions), 1)
        allowed = col <= start + token
        s = lax.dot_general(
            qbuf[:, :, lanes(k * HD, HD)].reshape(span, HD), kvbuf[0].reshape(positions, HD),
            (((1,), (1,)), ((), ())), preferred_element_type=jnp.float32,
        ) * scale
        s = jnp.where(allowed, s, NEG_FILL)
        p = jnp.exp(s - jnp.max(s, axis=1, keepdims=True))
        total = jnp.sum(p, axis=1, keepdims=True)
        o = jnp.dot(
            p.astype(jnp.bfloat16), kvbuf[1].reshape(positions, HD),
            preferred_element_type=jnp.float32,
        )
        attn[:, subl(c * pair, pair), lanes(x * width + k * HD, HD)] = (
            (o / total).astype(jnp.bfloat16).reshape(2, pair, HD)
        )

    piece = width // 4

    def attn_block(cc, xx, ch):
        return attn.at[:, subl(cc * pair, pair), lanes(xx * width + ch * piece, piece)]

    def attn_body(ch, carry):
        for k in range(piece // HD):
            head_body(ch * (piece // HD) + k)
        mine = attn_block(c, x, ch)
        remote(mine, mine, asx.at[ch], arx.at[ch], h, chip_peer).start()
        remote(mine, mine, asc.at[ch], arc.at[ch], h, core_peer).start()
        return carry

    lax.fori_loop(0, 4, attn_body, 0)

    def forward_body(ch, carry):
        far = attn_block(c, 1 - x, ch)
        remote(far, far, asx.at[ch], arx.at[ch], h, chip_peer).wait_recv()
        remote(far, far, asf.at[ch], arf.at[ch], h, core_peer).start()
        return carry

    lax.fori_loop(0, 4, forward_body, 0)

    def gathered_body(ch, carry):
        near = attn_block(1 - c, x, ch)
        far = attn_block(1 - c, 1 - x, ch)
        remote(near, near, asc.at[ch], arc.at[ch], h, core_peer).wait_recv()
        remote(far, far, asf.at[ch], arf.at[ch], h, core_peer).wait_recv()
        mine = attn_block(c, x, ch)
        remote(mine, mine, asx.at[ch], arx.at[ch], h, chip_peer).wait_send()
        remote(mine, mine, asc.at[ch], arc.at[ch], h, core_peer).wait_send()
        remote(mine, mine, asf.at[ch], arf.at[ch], h, core_peer).wait_send()
        return carry

    lax.fori_loop(0, 4, gathered_body, 0)
    wo_load.wait()
    res_load.wait()
    cols = 512

    def z_copy(half, d, n, ss, rs):
        hh = ring(d)
        at = lanes(n * cols, cols)
        slot = 3 * n + d - 1
        return remote(
            zsend.at[half, subl(hh * block, block), at], zrecv.at[half, d - 1, :, at],
            ss.at[half, slot], rs.at[half, slot], hh, r,
        )

    def project_body(half, carry):
        def chunk(n, inner):
            part = jnp.dot(
                attn[half], wo[:, lanes(n * cols, cols)], preferred_element_type=jnp.float32
            )
            zsend[half, :, lanes(n * cols, cols)] = part.astype(jnp.bfloat16)
            for d in (2, 1, 3):
                z_copy(half, d, n, zss, zrs).start()
            return inner

        lax.fori_loop(0, depth // cols, chunk, 0)
        return carry

    lax.fori_loop(0, 2, project_body, 0)
    wd1_load.start()

    def r_copy(half, d, source):
        mine = resid.at[half, subl(source * block, block), :]
        return remote(mine, mine, rss.at[half, d - 1], rrs.at[half, d - 1], ring(d), r)

    def resid_body(half, carry):
        def chunk(n, inner):
            at = lanes(n * cols, cols)
            total = zsend[half, subl(h * block, block), at].astype(jnp.float32)
            total = total + res[half, :, at].astype(jnp.float32)
            for d in (1, 2, 3):
                z_copy(half, d, n, zss, zrs).wait_recv()
                total = total + zrecv[half, d - 1, :, at].astype(jnp.float32)
            resid[half, subl(h * block, block), at] = total.astype(jnp.bfloat16)
            return inner

        lax.fori_loop(0, depth // cols, chunk, 0)
        for d in (2, 1, 3):
            r_copy(half, d, h).start()
        return carry

    lax.fori_loop(0, 2, resid_body, 0)
    wg_load.wait()
    wu_load.wait()

    def both(qi):
        at = lanes(qi * quarter, quarter)
        return (
            jnp.dot(scl[...], wg[:, at], preferred_element_type=jnp.float32),
            jnp.dot(scl[...], wu[:, at], preferred_element_type=jnp.float32),
        )

    def g_copy(half, xx):
        return remote(
            gsend.at[xx], grecv.at[half, xx], gss.at[half, xx], grs.at[half, xx], h, core_peer
        )

    def sq_copy(half):
        return remote(sqs.at[half], sqr.at[half], sss.at[half, 0], srs.at[half, 0], h, core_peer)

    def sq_copy2(half):
        return remote(sqr.at[half], sqx.at[half], sss.at[half, 1], srs.at[half, 1], h, chip_peer)

    def x_copy(half):
        return remote(grecv.at[half, 1 - x], xrecv.at[half], xss.at[half], xrs.at[half], h, chip_peer)

    def gate_body(half, carry):
        for d in (1, 2, 3):
            r_copy(half, d, lax.rem(h + 4 - d, 4)).wait_recv()
        wide = resid[half].astype(jnp.float32)
        sqs[half] = jnp.broadcast_to(jnp.sum(wide * wide, axis=1, keepdims=True), (span, 128))
        sq_copy(half).start()
        scl[...] = (wide * gain_ref[...]).astype(jnp.bfloat16)

        @pl.when(half == 1)
        def _():
            for xx in (0, 1):
                g_copy(0, xx).wait_send()

        def partner(xx):
            g, u = both(2 * xx + 1 - c)
            gsend[xx, :, 0:quarter] = g.astype(jnp.bfloat16)
            gsend[xx, :, quarter:] = u.astype(jnp.bfloat16)
            g_copy(half, xx).start()

        partner(1 - x)
        g, u = both(2 * (1 - x) + c)
        g_copy(half, 1 - x).wait_recv()
        grecv[half, 1 - x, :, 0:quarter] = (
            g + grecv[half, 1 - x, :, 0:quarter].astype(jnp.float32)
        ).astype(jnp.bfloat16)
        grecv[half, 1 - x, :, quarter:] = (
            u + grecv[half, 1 - x, :, quarter:].astype(jnp.float32)
        ).astype(jnp.bfloat16)
        x_copy(half).start()
        sq_copy(half).wait_recv()
        sqr[half] = sqs[half] + sqr[half]
        sq_copy2(half).start()
        partner(x)
        g, u = both(2 * x + c)
        g_copy(half, x).wait_recv()
        grecv[half, x, :, 0:quarter] = (
            g + grecv[half, x, :, 0:quarter].astype(jnp.float32)
        ).astype(jnp.bfloat16)
        grecv[half, x, :, quarter:] = (
            u + grecv[half, x, :, quarter:].astype(jnp.float32)
        ).astype(jnp.bfloat16)
        return carry

    lax.fori_loop(0, 2, gate_body, 0)

    def h_copy(half, owner, ss, rs, rr):
        mine = hid.at[half, :, lanes(owner * quarter, quarter)]
        return remote(mine, mine, ss.at[half], rs.at[half], h, rr)

    def hidden_body(half, carry):
        x_copy(half).wait_recv()
        sq_copy2(half).wait_recv()
        square = (sqr[half] + sqx[half])[:, 0:1]
        inverse = lax.rsqrt(square / D + EPSILON)
        summed = grecv[half, x].astype(jnp.float32) + xrecv[half].astype(jnp.float32)
        gate = summed[:, 0:quarter] * inverse
        up = summed[:, quarter:] * inverse
        hid[half, :, lanes(r * quarter, quarter)] = (gate / (1.0 + jnp.exp(-gate)) * up).astype(
            jnp.bfloat16
        )
        h_copy(half, r, hsx, hrx, chip_peer).start()
        h_copy(half, r, hsc, hrc, core_peer).start()
        return carry

    lax.fori_loop(0, 2, hidden_body, 0)
    wd1_load.wait()
    wd2_load.wait()

    def down_body(half, carry):
        h_copy(half, chip_peer, hsx, hrx, chip_peer).wait_recv()
        h_copy(half, chip_peer, hsf, hrf, core_peer).start()

        def sent(n, inner):
            for d in (1, 2, 3):
                z_copy(half, d, n, zss, zrs).wait_send()
            return inner

        lax.fori_loop(0, depth // cols, sent, 0)
        h_copy(half, core_peer, hsc, hrc, core_peer).wait_recv()
        h_copy(half, 2 * (1 - x) + 1 - c, hsf, hrf, core_peer).wait_recv()

        def chunk(n, inner):
            at = lanes(n * cols, cols)
            part = jnp.dot(
                hid[half, :, 0:first], wo[:, at], preferred_element_type=jnp.float32
            ) + jnp.dot(hid[half, :, first:], wd2[:, at], preferred_element_type=jnp.float32)
            zsend[half, :, at] = part.astype(jnp.bfloat16)
            for d in (2, 1, 3):
                z_copy(half, d, n, dss, drs).start()
            return inner

        lax.fori_loop(0, depth // cols, chunk, 0)
        return carry

    lax.fori_loop(0, 2, down_body, 0)

    def final_body(half, carry):
        def chunk(n, inner):
            at = lanes(n * cols, cols)
            total = zsend[half, subl(h * block, block), at].astype(jnp.float32)
            total = total + resid[half, subl(h * block, block), at].astype(jnp.float32)
            for d in (1, 2, 3):
                z_copy(half, d, n, dss, drs).wait_recv()
                total = total + zrecv[half, d - 1, :, at].astype(jnp.float32)
            out_ref[half, :, at] = total.astype(jnp.bfloat16)
            return inner

        lax.fori_loop(0, depth // cols, chunk, 0)
        return carry

    lax.fori_loop(0, 2, final_body, 0)

    @pl.when(sender)
    def _():
        for d in (1, 2, 3):
            q_copy(d).wait_send()

    kv_copy.wait_send()

    def drain(half, carry):
        for d in (1, 2, 3):
            r_copy(half, d, h).wait_send()
            for n in range(depth // cols):
                z_copy(half, d, n, dss, drs).wait_send()
        sq_copy(half).wait_send()
        sq_copy2(half).wait_send()
        x_copy(half).wait_send()
        h_copy(half, r, hsx, hrx, chip_peer).wait_send()
        h_copy(half, r, hsc, hrc, core_peer).wait_send()
        h_copy(half, chip_peer, hsf, hrf, core_peer).wait_send()
        return carry

    lax.fori_loop(0, 2, drain, 0)
    for xx in (0, 1):
        g_copy(1, xx).wait_send()


def fused(
    queries, kv_cache, start_positions, residual, out_weight, norm_gain, gate_weight, up_weight,
    down_weight,
):
    rows, wide = queries.shape
    block = rows // 2
    span = 4 * block
    width = wide // KVH
    depth = residual.shape[1]
    units = gate_weight.shape[1]
    quarter = units // 4
    first = out_weight.shape[0]
    half_rest = units - first
    bf, f32 = jnp.bfloat16, jnp.float32
    vmem, dma = pltpu.VMEM, pltpu.SemaphoreType.DMA
    anyspace = pl.BlockSpec(memory_space=pl.ANY)
    vspec = pl.BlockSpec(memory_space=pltpu.VMEM)
    out = pl.pallas_call(
        fused_kernel,
        out_shape=jax.ShapeDtypeStruct((2, block, depth), bf),
        in_specs=[
            anyspace, anyspace, pl.BlockSpec(memory_space=pltpu.SMEM), anyspace, anyspace, vspec,
            anyspace, anyspace, anyspace,
        ],
        out_specs=vspec,
        scratch_shapes=[
            vmem((first, depth), bf),
            vmem((depth, units), bf),
            vmem((depth, units), bf),
            vmem((half_rest, depth), bf),
            vmem((2, 2 * block, width), bf),
            vmem(kv_cache.shape, bf),
            vmem((2, span, 2 * width), bf),
            vmem((2, span, depth), bf),
            vmem((2, 3, block, depth), bf),
            vmem((2, span, depth), bf),
            vmem((2, block, depth), bf),
            vmem((span, depth), bf),
            vmem((2, span, 2 * quarter), bf),
            vmem((2, 2, span, 2 * quarter), bf),
            vmem((2, span, 2 * quarter), bf),
            vmem((2, span, units), bf),
            vmem((2, span, 128), f32),
            vmem((2, span, 128), f32),
            vmem((2, span, 128), f32),
            dma((8,)), dma((3,)), dma((2,)), dma((1,)), dma((1,)),
            dma((4,)), dma((4,)), dma((4,)), dma((4,)), dma((4,)), dma((4,)),
            dma((2, 12)), dma((2, 12)), dma((2, 3)), dma((2, 3)),
            dma((2, 2)), dma((2, 2)), dma((2,)), dma((2,)), dma((2, 2)), dma((2, 2)),
            dma((2,)), dma((2,)), dma((2,)), dma((2,)), dma((2,)), dma((2,)),
            dma((2, 12)), dma((2, 12)),
        ],
        compiler_params=pltpu.CompilerParams(
            collective_id=0, has_side_effects=True, vmem_limit_bytes=63 * 1024 * 1024
        ),
    )(
        queries.reshape(2, block, wide), kv_cache, start_positions,
        residual.reshape(2, block, depth), out_weight, norm_gain.reshape(1, depth), gate_weight,
        up_weight, down_weight,
    )
    return out.reshape(rows, depth)


def one_kernel_fits(mesh):
    return mesh.shape["heads"] == 4 and mesh.shape["rows"] == 4


def solution(mesh):
    return jax.shard_map(
        fused if one_kernel_fits(mesh) else local,
        mesh=mesh,
        in_specs=(
            P(("groups", "heads"), None),
            P(None, "groups", ("heads", "rows"), None),
            P("groups"),
            P(("groups", "heads"), "rows"),
            P("heads", "rows"),
            P("rows"),
            P("rows", "heads"),
            P("rows", "heads"),
            P("heads", "rows"),
        ),
        out_specs=P(("groups", "heads"), "rows"),
        check_vma=False,
    )
```
